32 devices in a mesh: nodes: 8 (over z, y), cols: 4 (over x, core).
Axes of the slice: x: 2, y: 2, z: 4, core: 2. Of those that a mesh axis runs over, the one named last changes fastest.
Arguments:
- vectors: bfloat16 [32, 4, 6, 16, 512], P('nodes', None, None, None, 'cols'), may hold values from -6 to 6
- node_shift: bfloat16 [32, 6, 16], P('nodes'), may hold values from 0.5 to 2
- coupling: float32 [4, 4], replicated, may hold values from -3 to 3
- dual_basis: bfloat16 [12288, 512], P(('nodes', 'cols')), may hold values from -0.0546875 to 0.0546875
Outputs:
- gram_matrix: float32 [512, 512], P('cols')
- rotated: bfloat16 [12288, 512], P(('nodes', 'cols'))
The draws below stay inside these ranges and needn't reach their ends.
All inputs are finite; a program needn't handle non-finite values.
Results may differ from the reference program's by a relative error of at most 0.0064.
Values may be sent and summed in bfloat16 or wider, within the bound.
A program may use at most 64 MiB of HBM per device.

```python
import math
import jax
import jax.numpy as jnp
from jax import lax

VECS = 512
DOFS = 4
GY = 6
GZ = 16
NX = 32
ROWS = 12288


def levels(stream_key, shape, pieces, least, high):
    gain, own = 1.0, jax.random.fold_in(stream_key, 6)
    for axis_at, blocks in pieces:
        heights = jnp.exp(jax.random.uniform(jax.random.fold_in(own, axis_at), (blocks,), jnp.float32, least / len(pieces), high / len(pieces)))
        gain = gain * jnp.repeat(heights, shape[axis_at] // blocks).reshape([-1 if axis == axis_at else 1 for axis in range(len(shape))])
    return gain


def bell_draw(rng, extent, width, reach, shards=(), dtype=jnp.bfloat16):
    entries = jax.random.normal(rng, extent, jnp.float32) * width
    if len(shards) > 0:
        entries = levels(rng, extent, shards, -0.22, 0.18) * entries
    return jnp.clip(entries, min=-reach, max=reach).astype(dtype)


def setup_inputs(seed: int = 0) -> dict:
    splits = jax.random.split(jax.random.key(seed), 5)
    return {
        "vectors": bell_draw(splits[0], (NX, DOFS, GY, GZ, VECS), 1.0, 6.0, ((0, 8), (4, 4))),
        "node_shift": jnp.clip(0.5 + 1.5 * jax.random.uniform(splits[1], (NX, GY, GZ), jnp.float32) ** levels(splits[1], (NX, GY, GZ), ((0, 8),), -0.2, 0.2), 0.5, 2.0).astype(jnp.bfloat16),
        "coupling": bell_draw(splits[2], (DOFS, DOFS), 1.0, 3.0, (), jnp.float32),
        "dual_basis": bell_draw(splits[3], (ROWS, VECS), ROWS ** -0.5, 0.0546875, ((0, 32),)),
    }


center_value = 10.0
half_width = 7.0


def operate(field_in, shift_full, coupling):
    padded = jnp.pad(field_in, ((1, 1), (0, 0), (1, 1), (1, 1), (0, 0)))
    beside = padded[2:, :, 1:-1, 1:-1] + padded[:-2, :, 1:-1, 1:-1]
    beside = beside + padded[1:-1, :, 2:, 1:-1] + padded[1:-1, :, :-2, 1:-1]
    beside = beside + padded[1:-1, :, 1:-1, 2:] + padded[1:-1, :, 1:-1, :-2]
    coupled = jnp.einsum('de,xeyzc->xdyzc', coupling, field_in, precision=lax.Precision.HIGHEST)
    return (6.0 + shift_full[:, None, :, :, None]) * field_in - beside + coupled


def reference(vectors, node_shift, coupling, dual_basis):
    shift_full = node_shift.astype(jnp.float32)
    block_width = math.gcd(VECS, 64)
    count_blocks = VECS // block_width
    split_cols = vectors.reshape(NX, DOFS, GY, GZ, count_blocks, block_width)
    split_cols = jnp.moveaxis(split_cols, 4, 0)

    def filter_block(col_block):
        state_zero = col_block.astype(jnp.float32)
        state_one = (operate(state_zero, shift_full, coupling) - center_value * state_zero) / half_width
        state_two = 2.0 * (operate(state_one, shift_full, coupling) - center_value * state_one) / half_width - state_zero
        state_three = 2.0 * (operate(state_two, shift_full, coupling) - center_value * state_two) / half_width - state_one
        return state_three.astype(jnp.bfloat16)

    filtered = lax.map(filter_block, split_cols)
    filtered = jnp.moveaxis(filtered, 0, 4).reshape(ROWS, VECS)
    gram_matrix = lax.dot_general(dual_basis, filtered, (((0,), (0,)), ((), ())), preferred_element_type=jnp.float32)
    gram_half = gram_matrix.astype(jnp.bfloat16)
    rotated = jnp.dot(filtered, gram_half, preferred_element_type=jnp.float32) * (VECS ** -0.5)
    return gram_matrix, rotated.astype(jnp.bfloat16)
```

```python
import functools

import jax
import jax.numpy as jnp
from jax import lax
from jax.experimental import pallas as pl
from jax.experimental.pallas import tpu as pltpu
from jax.sharding import PartitionSpec as P

center_value = 10.0
half_width = 7.0
MESH = pl.DeviceIdType.MESH
WIDTH = 3


def with_halo(block, sides, width):
    for axis, dim in sides:
        count = lax.axis_size(axis)
        forward = [(i, i + 1) for i in range(count - 1)]
        backward = [(target, source) for source, target in forward]
        low = lax.ppermute(
            lax.slice_in_dim(block, block.shape[dim] - width, None, axis=dim), axis, forward
        )
        high = lax.ppermute(lax.slice_in_dim(block, 0, width, axis=dim), axis, backward)
        block = jnp.concatenate([low, block, high], axis=dim)
    return block


def operate_inner(padded, shift_part, coupling):
    middle = padded[1:-1]
    beside = padded[2:] + padded[:-2]
    spread = jnp.pad(middle, ((0, 0), (0, 0), (1, 1), (1, 1), (0, 0)))
    beside = beside + spread[:, :, 2:, 1:-1] + spread[:, :, :-2, 1:-1]
    beside = beside + spread[:, :, 1:-1, 2:] + spread[:, :, 1:-1, :-2]
    coupled = jnp.einsum("de,xeyzc->xdyzc", coupling, middle, precision=lax.Precision.HIGHEST)
    return (6.0 + shift_part[:, None, :, :, None]) * middle - beside + coupled


def shards_plain(vectors, node_shift, coupling, dual_basis):
    shift_full = node_shift.astype(jnp.float32)

    def advance(state):
        padded = with_halo(state, (("nodes", 0),), 1)
        return operate_inner(padded, shift_full, coupling) - center_value * state

    state_zero = vectors.astype(jnp.float32)
    state_one = advance(state_zero) / half_width
    state_two = 2.0 * advance(state_one) / half_width - state_zero
    state_three = 2.0 * advance(state_two) / half_width - state_one
    filtered = state_three.astype(jnp.bfloat16).reshape(-1, state_three.shape[-1])
    row_stack = lax.all_to_all(filtered, "cols", split_axis=0, concat_axis=1, tiled=True)
    partial_gram = lax.dot_general(
        dual_basis, row_stack, (((0,), (0,)), ((), ())), preferred_element_type=jnp.float32
    )
    vector_count = dual_basis.shape[1]
    own_rows = lax.psum_scatter(partial_gram, "cols", scatter_dimension=0, tiled=True)
    own_rows = lax.psum(own_rows, "nodes")
    rotated_sum = jnp.dot(
        row_stack,
        lax.all_gather(own_rows.astype(jnp.bfloat16), "cols", axis=0, tiled=True),
        preferred_element_type=jnp.float32,
    )
    rotated = (rotated_sum * vector_count ** (-0.5)).astype(jnp.bfloat16)
    return (own_rows, rotated)


def remote(src, dst, send, recv, node, col):
    return pltpu.make_async_remote_copy(
        src_ref=src, dst_ref=dst, send_sem=send, recv_sem=recv,
        device_id=(node, col), device_id_type=MESH,
    )


def kernel(
    nodes, cols, v_ref, shift_ref, c_ref, d_ref, gram_ref, rot_ref,
    ghost, s0, s1, s2, shc, shb, dall, filt, frow, gacc, gsend, rsbuf, gall,
    halo_send, halo_recv, sh_send, sh_recv, d_send, d_recv, df_send, own_sem,
    f_send, f_recv, rs_send, rs_recv, ag_send, ag_recv, fw_send, fw_recv,
):
    n = lax.axis_index("nodes")
    c = lax.axis_index("cols")
    layers, dofs, gy, gz, width = v_ref.shape
    slab_rows = dofs * gy * gz
    own_rows, vecs = d_ref.shape
    piece = width // nodes
    sib = c + 1 - 2 * lax.rem(c, 2)
    pairs = cols // 2
    has_lo = n > 0
    has_hi = n < nodes - 1

    def wrap(value, count):
        return lax.rem(value + count, count)

    barrier = pltpu.get_barrier_semaphore()
    partners = []
    for dn in range(nodes):
        for dc in range(pairs):
            if dn or dc:
                partners.append((wrap(n + dn, nodes), wrap(c + 2 * dc, cols)))
    for dc in range(pairs):
        partners.append((n, wrap(sib + 2 * dc, cols)))
    for partner in partners:
        pl.semaphore_signal(barrier, inc=1, device_id=partner, device_id_type=MESH)

    own_d = pltpu.make_async_copy(
        d_ref, dall.at[pl.ds(pl.multiple_of(c * own_rows, 16), own_rows)], own_sem.at[0]
    )
    own_d.start()
    shc[2:layers + 2] = jnp.zeros_like(shc[2:layers + 2])
    for l in range(layers):
        shc[l + 2, 0:gy, 0:gz] = shift_ref[l].astype(jnp.float32)
    pl.semaphore_wait(barrier, len(partners))

    def up_copy(k):
        return remote(v_ref.at[layers - 1 - k], ghost.at[k], halo_send.at[k], halo_recv.at[k], n + 1, c)

    def down_copy(k):
        return remote(
            v_ref.at[k], ghost.at[WIDTH + k], halo_send.at[WIDTH + k], halo_recv.at[WIDTH + k], n - 1, c
        )

    def up_shift():
        return remote(shc.at[pl.ds(layers, 2)], shc.at[pl.ds(0, 2)], sh_send.at[0], sh_recv.at[0], n + 1, c)

    def down_shift():
        return remote(
            shc.at[pl.ds(2, 2)], shc.at[pl.ds(layers + 2, 2)], sh_send.at[1], sh_recv.at[1], n - 1, c
        )

    @pl.when(has_hi)
    def _():
        up_copy(0).start()
        up_shift().start()

    @pl.when(has_lo)
    def _():
        down_copy(0).start()
        down_shift().start()

    for k in range(1, WIDTH):
        @pl.when(has_hi)
        def _(k=k):
            up_copy(k).start()

        @pl.when(has_lo)
        def _(k=k):
            down_copy(k).start()

    def d_rows(q):
        return dall.at[pl.ds(pl.multiple_of(q * own_rows, 16), own_rows)]

    def d_copy(j):
        target = sib if j == 0 else wrap(c + 2 * j, cols)
        return remote(d_ref, d_rows(c), d_send.at[j], d_recv.at[j], n, target)

    def d_forward(j):
        source = wrap(c - 2 * j, cols)
        return remote(d_rows(source), d_rows(source), df_send.at[j], d_recv.at[pairs + j], n, sib)

    for j in list(range(1, pairs)) + [0]:
        d_copy(j).start()

    s0[:, :, 0] = jnp.zeros_like(s0[:, :, 0])
    s0[:, :, gy + 1] = jnp.zeros_like(s0[:, :, 0])
    s1[:, :, 0] = jnp.zeros_like(s1[:, :, 0])
    s1[:, :, gy + 1] = jnp.zeros_like(s1[:, :, 0])
    s2[:, :, 0] = jnp.zeros_like(s2[:, :, 0])
    s2[:, :, gy + 1] = jnp.zeros_like(s2[:, :, 0])

    @pl.when(jnp.logical_not(has_lo))
    def _():
        s0[0:3] = jnp.zeros_like(s0[0:3])
        s1[0:2] = jnp.zeros_like(s1[0:2])
        s2[0:1] = jnp.zeros_like(s2[0:1])

    @pl.when(jnp.logical_not(has_hi))
    def _():
        s0[layers + 3:] = jnp.zeros_like(s0[0:3])
        s1[layers + 2:] = jnp.zeros_like(s1[0:2])
        s2[layers + 1:] = jnp.zeros_like(s2[0:1])

    row_id = lax.broadcasted_iota(jnp.int32, (gz, width), 0)
    eye = lax.broadcasted_iota(jnp.int32, (gz, gz), 0) == lax.broadcasted_iota(jnp.int32, (gz, gz), 1)

    def spread(l):
        for y in range(gy):
            row = jnp.broadcast_to(shc[l + 2, y:y + 1, 0:gz], (gz, gz))
            column = jnp.sum(jnp.where(eye, row, 0.0), axis=1, keepdims=True)
            shb[l + 2, y] = jnp.broadcast_to(column + (6.0 - center_value), (gz, width))

    def load(target, block):
        s0[target, :, 1:gy + 1] = block.astype(jnp.float32)

    def beside(mid):
        down = jnp.where(row_id > 0, pltpu.roll(mid, 1, 0), 0.0)
        up = jnp.where(row_id < gz - 1, pltpu.roll(mid, gz - 1, 0), 0.0)
        return down + up

    coef = [[c_ref[d, e] for e in range(dofs)] for d in range(dofs)]

    def stencil(src, at, l, scale, y):
        mids = [src[at, e, y + 1] for e in range(dofs)]
        base = shb[l + 2, y]
        out = []
        for d in range(dofs):
            near = src[at - 1, d, y + 1] + src[at + 1, d, y + 1]
            near = near + (src[at, d, y] + src[at, d, y + 2]) + beside(mids[d])
            total = (base + coef[d][d]) * mids[d] - near
            for e in range(dofs):
                if e != d:
                    total = total + coef[d][e] * mids[e]
            out.append(total * scale)
        return out

    def one(l):
        @pl.loop(0, gy)
        def _(y):
            for d, value in enumerate(stencil(s0, l + 3, l, 1.0 / half_width, y)):
                s1[l + 2, d, y + 1] = value

    def two(l):
        @pl.loop(0, gy)
        def _(y):
            for d, value in enumerate(stencil(s1, l + 2, l, 2.0 / half_width, y)):
                s2[l + 1, d, y + 1] = value - s0[l + 3, d, y + 1]

    def three(l):
        @pl.loop(0, gy)
        def _(y):
            for d, value in enumerate(stencil(s2, l + 1, l, 2.0 / half_width, y)):
                value = value - s1[l + 2, d, y + 1]
                at = pl.multiple_of(l * slab_rows + (d * gy + y) * gz, 16)
                filt[pl.ds(at, gz), :] = value.astype(filt.dtype)

    inner = range(1, layers - 1)
    ends = (0, layers - 1)

    for l in range(layers):
        load(l + 3, v_ref[l])
        spread(l)
    for l in inner:
        one(l)

    @pl.when(has_lo)
    def _():
        up_copy(0).wait_recv()
        load(2, ghost[0])
        up_shift().wait_recv()
        spread(-1)
        spread(-2)

    @pl.when(has_hi)
    def _():
        down_copy(0).wait_recv()
        load(layers + 3, ghost[WIDTH])
        down_shift().wait_recv()
        spread(layers)
        spread(layers + 1)

    for l in ends:
        one(l)
    for l in inner:
        two(l)

    @pl.when(has_lo)
    def _():
        up_copy(1).wait_recv()
        load(1, ghost[1])
        one(-1)

    @pl.when(has_hi)
    def _():
        down_copy(1).wait_recv()
        load(layers + 4, ghost[WIDTH + 1])
        one(layers)

    for l in ends:
        two(l)
    for l in inner:
        three(l)

    for j in range(1, pairs):
        d_copy(j).wait_recv()
        d_forward(j).start()

    @pl.when(has_lo)
    def _():
        up_copy(2).wait_recv()
        load(0, ghost[2])
        one(-2)
        two(-1)

    @pl.when(has_hi)
    def _():
        down_copy(2).wait_recv()
        load(layers + 5, ghost[WIDTH + 2])
        one(layers + 1)
        two(layers)

    for l in ends:
        three(l)

    own_d.wait()
    d_copy(0).wait_recv()
    for j in range(1, pairs):
        d_forward(j).wait_recv()
    gacc[...] = lax.dot_general(
        filt[...], dall[...], (((0,), (0,)), ((), ())), preferred_element_type=jnp.float32
    )
    gsend[...] = gacc[...].astype(gsend.dtype)

    def rs_copy(j):
        target = wrap(n + j, nodes)
        return remote(
            gsend.at[pl.ds(pl.multiple_of(target * piece, 16), piece)],
            rsbuf.at[j - 1], rs_send.at[j - 1], rs_recv.at[j - 1], target, c,
        )

    for j in range(1, nodes):
        rs_copy(j).start()

    def f_copy(j):
        target = wrap(c + j, cols)
        return remote(
            filt.at[pl.ds(pl.multiple_of(target * own_rows, 16), own_rows)],
            frow.at[:, pl.ds(pl.multiple_of(c * width, 128), width)],
            f_send.at[j - 1], f_recv.at[j - 1], n, target,
        )

    for j in range(1, cols):
        f_copy(j).start()
    own_f = pltpu.make_async_copy(
        filt.at[pl.ds(pl.multiple_of(c * own_rows, 16), own_rows)],
        frow.at[:, pl.ds(pl.multiple_of(c * width, 128), width)],
        own_sem.at[1],
    )
    own_f.start()

    total = gacc[pl.ds(pl.multiple_of(n * piece, 16), piece), :]
    for j in range(1, nodes):
        rs_copy(j).wait_recv()
        total = total + rsbuf[j - 1].astype(jnp.float32)

    def g_rows(node, col):
        return gall.at[pl.ds(pl.multiple_of(col * width + node * piece, 16), piece)]

    gall[pl.ds(pl.multiple_of(c * width + n * piece, 16), piece), :] = total.astype(gall.dtype)

    def ag_copy(dn, dc):
        slot = dn * pairs + dc
        return remote(
            g_rows(n, c), g_rows(n, c), ag_send.at[slot], ag_recv.at[slot],
            wrap(n + dn, nodes), wrap(c + 2 * dc, cols),
        )

    def fw_copy(dn, dc):
        slot = dn * pairs + dc
        rows = g_rows(wrap(n - dn, nodes), wrap(c - 2 * dc, cols))
        return remote(rows, rows, fw_send.at[slot], fw_recv.at[slot], n, sib)

    steps = [(dn, dc) for dn in range(nodes) for dc in range(pairs)]
    fw_copy(0, 0).start()
    for dn, dc in steps[1:]:
        ag_copy(dn, dc).start()
    for dn, dc in steps[1:]:
        ag_copy(dn, dc).wait_recv()
        fw_copy(dn, dc).start()
    own_f.wait()
    for j in range(1, cols):
        f_copy(j).wait_recv()
    for dn, dc in steps:
        fw_copy(dn, dc).wait_recv()

    rotated = lax.dot_general(
        frow[...], gall[...], (((1,), (1,)), ((), ())), preferred_element_type=jnp.float32
    )
    rot_ref[...] = (rotated * vecs ** (-0.5)).astype(rot_ref.dtype)
    unit = (
        lax.broadcasted_iota(jnp.int32, (width, width), 0)
        == lax.broadcasted_iota(jnp.int32, (width, width), 1)
    ).astype(jnp.float32).astype(gall.dtype)
    gram_ref[...] = lax.dot_general(
        unit, gall[:, pl.ds(pl.multiple_of(c * width, 128), width)],
        (((1,), (1,)), ((), ())), preferred_element_type=jnp.float32,
    )

    @pl.when(has_hi)
    def _():
        for k in range(WIDTH):
            up_copy(k).wait_send()
        up_shift().wait_send()

    @pl.when(has_lo)
    def _():
        for k in range(WIDTH):
            down_copy(k).wait_send()
        down_shift().wait_send()

    for j in range(pairs):
        d_copy(j).wait_send()
    for j in range(1, pairs):
        d_forward(j).wait_send()
    for j in range(1, cols):
        f_copy(j).wait_send()
    for j in range(1, nodes):
        rs_copy(j).wait_send()
    for dn, dc in steps[1:]:
        ag_copy(dn, dc).wait_send()
    for dn, dc in steps:
        fw_copy(dn, dc).wait_send()


def shards_fused(nodes, cols, vectors, node_shift, coupling, dual_basis):
    layers, dofs, gy, gz, width = vectors.shape
    own_rows, vecs = dual_basis.shape
    slab = layers * dofs * gy * gz
    piece = width // nodes
    pairs = cols // 2
    f32, bf16 = jnp.float32, jnp.bfloat16
    dma = pltpu.SemaphoreType.DMA
    vmem = pl.BlockSpec(memory_space=pltpu.VMEM)
    return pl.pallas_call(
        functools.partial(kernel, nodes, cols),
        out_shape=(
            jax.ShapeDtypeStruct((vecs // cols, vecs), f32),
            jax.ShapeDtypeStruct((own_rows, vecs), bf16),
        ),
        in_specs=[vmem, vmem, pl.BlockSpec(memory_space=pltpu.SMEM), vmem],
        out_specs=(vmem, vmem),
        scratch_shapes=[
            pltpu.VMEM((2 * WIDTH, dofs, gy, gz, width), bf16),
            pltpu.VMEM((layers + 6, dofs, gy + 2, gz, width), f32),
            pltpu.VMEM((layers + 4, dofs, gy + 2, gz, width), f32),
            pltpu.VMEM((layers + 2, dofs, gy + 2, gz, width), f32),
            pltpu.VMEM((layers + 4, 8, 128), f32),
            pltpu.VMEM((layers + 4, gy, gz, width), f32),
            pltpu.VMEM((slab, vecs), bf16),
            pltpu.VMEM((slab, width), bf16),
            pltpu.VMEM((own_rows, vecs), bf16),
            pltpu.VMEM((width, vecs), f32),
            pltpu.VMEM((width, vecs), bf16),
            pltpu.VMEM((nodes - 1, piece, vecs), bf16),
            pltpu.VMEM((vecs, vecs), bf16),
            dma((2 * WIDTH,)), dma((2 * WIDTH,)), dma((2,)), dma((2,)),
            dma((pairs,)), dma((2 * pairs,)), dma((pairs,)), dma((2,)),
            dma((cols - 1,)), dma((cols - 1,)), dma((nodes - 1,)), dma((nodes - 1,)),
            dma((nodes * pairs,)), dma((nodes * pairs,)), dma((nodes * pairs,)), dma((nodes * pairs,)),
        ],
        compiler_params=pltpu.CompilerParams(
            collective_id=0, has_side_effects=True, vmem_limit_bytes=40 * 1024 * 1024
        ),
        cost_estimate=pl.CostEstimate(flops=4 * own_rows * vecs * vecs, bytes_accessed=4 << 20, transcendentals=0),
    )(vectors, node_shift, coupling, dual_basis)


def shards(nodes, cols, vectors, node_shift, coupling, dual_basis):
    layers, dofs, gy, gz, width = vectors.shape
    own_rows = dual_basis.shape[0]
    fits = (
        width % (16 * nodes) == 0 and width % 128 == 0 and gz == 16 and gy <= 8 and layers >= WIDTH
        and cols % 2 == 0 and own_rows % 16 == 0 and own_rows * cols == layers * dofs * gy * gz
    )
    if fits:
        return shards_fused(nodes, cols, vectors, node_shift, coupling, dual_basis)
    return shards_plain(vectors, node_shift, coupling, dual_basis)


def solution(mesh):
    placed = (
        P("nodes", None, None, None, "cols"),
        P("nodes", None, None),
        P(),
        P(("nodes", "cols"), None),
    )
    return jax.shard_map(
        functools.partial(shards, mesh.shape["nodes"], mesh.shape["cols"]),
        mesh=mesh,
        in_specs=placed,
        out_specs=(P("cols", None), P(("nodes", "cols"), None)),
        check_vma=False,
    )
```

```python
import functools

import jax
import jax.numpy as jnp
from jax import lax
from jax.experimental import pallas as pl
from jax.experimental.pallas import tpu as pltpu
from jax.sharding import PartitionSpec as P

center_value = 10.0
half_width = 7.0
MESH = pl.DeviceIdType.MESH
WIDTH = 3


def with_halo(block, sides, width):
    for axis, dim in sides:
        count = lax.axis_size(axis)
        forward = [(i, i + 1) for i in range(count - 1)]
        backward = [(target, source) for source, target in forward]
        low = lax.ppermute(
            lax.slice_in_dim(block, block.shape[dim] - width, None, axis=dim), axis, forward
        )
        high = lax.ppermute(lax.slice_in_dim(block, 0, width, axis=dim), axis, backward)
        block = jnp.concatenate([low, block, high], axis=dim)
    return block


def operate_inner(padded, shift_part, coupling):
    middle = padded[1:-1]
    beside = padded[2:] + padded[:-2]
    spread = jnp.pad(middle, ((0, 0), (0, 0), (1, 1), (1, 1), (0, 0)))
    beside = beside + spread[:, :, 2:, 1:-1] + spread[:, :, :-2, 1:-1]
    beside = beside + spread[:, :, 1:-1, 2:] + spread[:, :, 1:-1, :-2]
    coupled = jnp.einsum("de,xeyzc->xdyzc", coupling, middle, precision=lax.Precision.HIGHEST)
    return (6.0 + shift_part[:, None, :, :, None]) * middle - beside + coupled


def shards_plain(vectors, node_shift, coupling, dual_basis):
    shift_full = node_shift.astype(jnp.float32)

    def advance(state):
        padded = with_halo(state, (("nodes", 0),), 1)
        return operate_inner(padded, shift_full, coupling) - center_value * state

    state_zero = vectors.astype(jnp.float32)
    state_one = advance(state_zero) / half_width
    state_two = 2.0 * advance(state_one) / half_width - state_zero
    state_three = 2.0 * advance(state_two) / half_width - state_one
    filtered = state_three.astype(jnp.bfloat16).reshape(-1, state_three.shape[-1])
    row_stack = lax.all_to_all(filtered, "cols", split_axis=0, concat_axis=1, tiled=True)
    partial_gram = lax.dot_general(
        dual_basis, row_stack, (((0,), (0,)), ((), ())), preferred_element_type=jnp.float32
    )
    vector_count = dual_basis.shape[1]
    own_rows = lax.psum_scatter(partial_gram, "cols", scatter_dimension=0, tiled=True)
    own_rows = lax.psum(own_rows, "nodes")
    rotated_sum = jnp.dot(
        row_stack,
        lax.all_gather(own_rows.astype(jnp.bfloat16), "cols", axis=0, tiled=True),
        preferred_element_type=jnp.float32,
    )
    rotated = (rotated_sum * vector_count ** (-0.5)).astype(jnp.bfloat16)
    return (own_rows, rotated)


def remote(src, dst, send, recv, node, col):
    return pltpu.make_async_remote_copy(
        src_ref=src, dst_ref=dst, send_sem=send, recv_sem=recv,
        device_id=(node, col), device_id_type=MESH,
    )


def kernel(
    nodes, cols, v_hbm, shift_ref, c_ref, d_hbm, frow, gall,
    v_ref, ghost, s0, s1, s2, shc, shb, dall, filt, gacc, gsend, rsbuf,
    halo_send, halo_recv, sh_send, sh_recv, d_send, d_recv, df_send, own_sem,
    f_send, f_recv, rs_send, rs_recv, ag_send, ag_recv, fw_send, fw_recv,
):
    n = lax.axis_index("nodes")
    c = lax.axis_index("cols")
    layers, dofs, gy, gz, width = v_ref.shape
    slab_rows = dofs * gy * gz
    own_rows, vecs = d_hbm.shape
    piece = width // nodes
    sib = c + 1 - 2 * lax.rem(c, 2)
    pairs = cols // 2
    has_lo = n > 0
    has_hi = n < nodes - 1

    def wrap(value, count):
        return lax.rem(value + count, count)

    barrier = pltpu.get_barrier_semaphore()
    partners = []
    for dn in range(nodes):
        for dc in range(pairs):
            if dn or dc:
                partners.append((wrap(n + dn, nodes), wrap(c + 2 * dc, cols)))
    for dc in range(pairs):
        partners.append((n, wrap(sib + 2 * dc, cols)))
    for partner in partners:
        pl.semaphore_signal(barrier, inc=1, device_id=partner, device_id_type=MESH)

    own_v = pltpu.make_async_copy(v_hbm, v_ref, own_sem.at[2])
    own_v.start()
    own_d = pltpu.make_async_copy(
        d_hbm, dall.at[pl.ds(pl.multiple_of(c * own_rows, 16), own_rows)], own_sem.at[0]
    )
    own_d.start()
    shc[2:layers + 2] = jnp.zeros_like(shc[2:layers + 2])
    for l in range(layers):
        shc[l + 2, 0:gy, 0:gz] = shift_ref[:, l].astype(jnp.float32)
    s0[:, :, 0] = jnp.zeros_like(s0[:, :, 0])
    s0[:, :, gy + 1] = jnp.zeros_like(s0[:, :, 0])
    s1[:, :, 0] = jnp.zeros_like(s1[:, :, 0])
    s1[:, :, gy + 1] = jnp.zeros_like(s1[:, :, 0])
    s2[:, :, 0] = jnp.zeros_like(s2[:, :, 0])
    s2[:, :, gy + 1] = jnp.zeros_like(s2[:, :, 0])

    @pl.when(jnp.logical_not(has_lo))
    def _():
        s0[0:3] = jnp.zeros_like(s0[0:3])
        s1[0:2] = jnp.zeros_like(s1[0:2])
        s2[0:1] = jnp.zeros_like(s2[0:1])

    @pl.when(jnp.logical_not(has_hi))
    def _():
        s0[layers + 3:] = jnp.zeros_like(s0[0:3])
        s1[layers + 2:] = jnp.zeros_like(s1[0:2])
        s2[layers + 1:] = jnp.zeros_like(s2[0:1])

    row_id = lax.broadcasted_iota(jnp.int32, (gz, width), 0)
    eye = lax.broadcasted_iota(jnp.int32, (gz, gz), 0) == lax.broadcasted_iota(jnp.int32, (gz, gz), 1)

    def spread(l):
        for y in range(gy):
            row = jnp.broadcast_to(shc[l + 2, y:y + 1, 0:gz], (gz, gz))
            column = jnp.sum(jnp.where(eye, row, 0.0), axis=1, keepdims=True)
            shb[l + 2, y] = jnp.broadcast_to(column + (6.0 - center_value), (gz, width))

    def load(target, block):
        s0[target, :, 1:gy + 1] = block.astype(jnp.float32)

    def beside(mid):
        down = jnp.where(row_id > 0, pltpu.roll(mid, 1, 0), 0.0)
        up = jnp.where(row_id < gz - 1, pltpu.roll(mid, gz - 1, 0), 0.0)
        return down + up

    coef = [[c_ref[d, e] for e in range(dofs)] for d in range(dofs)]

    def stencil(src, at, l, scale, y):
        mids = [src[at, e, y + 1] for e in range(dofs)]
        base = shb[l + 2, y]
        out = []
        for d in range(dofs):
            near = src[at - 1, d, y + 1] + src[at + 1, d, y + 1]
            near = near + (src[at, d, y] + src[at, d, y + 2]) + beside(mids[d])
            total = (base + coef[d][d]) * mids[d] - near
            for e in range(dofs):
                if e != d:
                    total = total + coef[d][e] * mids[e]
            out.append(total * scale)
        return out

    def one(l):
        @pl.loop(0, gy)
        def _(y):
            for d, value in enumerate(stencil(s0, l + 3, l, 1.0 / half_width, y)):
                s1[l + 2, d, y + 1] = value

    def two(l):
        @pl.loop(0, gy)
        def _(y):
            for d, value in enumerate(stencil(s1, l + 2, l, 2.0 / half_width, y)):
                s2[l + 1, d, y + 1] = value - s0[l + 3, d, y + 1]

    def three(l):
        @pl.loop(0, gy)
        def _(y):
            for d, value in enumerate(stencil(s2, l + 1, l, 2.0 / half_width, y)):
                value = value - s1[l + 2, d, y + 1]
                at = pl.multiple_of(l * slab_rows + (d * gy + y) * gz, 16)
                filt[pl.ds(at, gz), :] = value.astype(filt.dtype)

    inner = range(1, layers - 1)
    ends = (0, layers - 1)

    own_v.wait()
    for l in range(layers):
        load(l + 3, v_ref[l])
        spread(l)
    own_d.wait()
    for l in inner:
        one(l)
    pl.semaphore_wait(barrier, len(partners))

    def up_copy(k):
        return remote(v_ref.at[layers - 1 - k], ghost.at[k], halo_send.at[k], halo_recv.at[k], n + 1, c)

    def down_copy(k):
        return remote(
            v_ref.at[k], ghost.at[WIDTH + k], halo_send.at[WIDTH + k], halo_recv.at[WIDTH + k], n - 1, c
        )

    def up_shift():
        return remote(shc.at[pl.ds(layers, 2)], shc.at[pl.ds(0, 2)], sh_send.at[0], sh_recv.at[0], n + 1, c)

    def down_shift():
        return remote(
            shc.at[pl.ds(2, 2)], shc.at[pl.ds(layers + 2, 2)], sh_send.at[1], sh_recv.at[1], n - 1, c
        )

    @pl.when(has_hi)
    def _():
        up_copy(0).start()
        up_shift().start()

    @pl.when(has_lo)
    def _():
        down_copy(0).start()
        down_shift().start()

    for k in range(1, WIDTH):
        @pl.when(has_hi)
        def _(k=k):
            up_copy(k).start()

        @pl.when(has_lo)
        def _(k=k):
            down_copy(k).start()

    def d_rows(q):
        return dall.at[pl.ds(pl.multiple_of(q * own_rows, 16), own_rows)]

    def d_copy(j):
        target = sib if j == 0 else wrap(c + 2 * j, cols)
        return remote(d_rows(c), d_rows(c), d_send.at[j], d_recv.at[j], n, target)

    def d_forward(j):
        source = wrap(c - 2 * j, cols)
        return remote(d_rows(source), d_rows(source), df_send.at[j], d_recv.at[pairs + j], n, sib)

    for j in list(range(1, pairs)) + [0]:
        d_copy(j).start()

    @pl.when(has_lo)
    def _():
        up_copy(0).wait_recv()
        load(2, ghost[0])
        up_shift().wait_recv()
        spread(-1)
        spread(-2)

    @pl.when(has_hi)
    def _():
        down_copy(0).wait_recv()
        load(layers + 3, ghost[WIDTH])
        down_shift().wait_recv()
        spread(layers)
        spread(layers + 1)

    for l in ends:
        one(l)
    for l in inner:
        two(l)

    @pl.when(has_lo)
    def _():
        up_copy(1).wait_recv()
        load(1, ghost[1])
        one(-1)

    @pl.when(has_hi)
    def _():
        down_copy(1).wait_recv()
        load(layers + 4, ghost[WIDTH + 1])
        one(layers)

    for l in ends:
        two(l)
    for l in inner:
        three(l)

    for j in range(1, pairs):
        d_copy(j).wait_recv()
        d_forward(j).start()

    @pl.when(has_lo)
    def _():
        up_copy(2).wait_recv()
        load(0, ghost[2])
        one(-2)
        two(-1)

    @pl.when(has_hi)
    def _():
        down_copy(2).wait_recv()
        load(layers + 5, ghost[WIDTH + 2])
        one(layers + 1)
        two(layers)

    for l in ends:
        three(l)

    d_copy(0).wait_recv()
    for j in range(1, pairs):
        d_forward(j).wait_recv()
    gacc[...] = lax.dot_general(
        filt[...], dall[...], (((0,), (0,)), ((), ())), preferred_element_type=jnp.float32
    )
    gsend[...] = gacc[...].astype(gsend.dtype)

    def rs_copy(j):
        target = wrap(n + j, nodes)
        return remote(
            gsend.at[pl.ds(pl.multiple_of(target * piece, 16), piece)],
            rsbuf.at[j - 1], rs_send.at[j - 1], rs_recv.at[j - 1], target, c,
        )

    for j in range(1, nodes):
        rs_copy(j).start()

    def f_copy(j):
        target = wrap(c + j, cols)
        return remote(
            filt.at[pl.ds(pl.multiple_of(target * own_rows, 16), own_rows)],
            frow.at[:, pl.ds(pl.multiple_of(c * width, 128), width)],
            f_send.at[j - 1], f_recv.at[j - 1], n, target,
        )

    for j in range(1, cols):
        f_copy(j).start()
    own_f = pltpu.make_async_copy(
        filt.at[pl.ds(pl.multiple_of(c * own_rows, 16), own_rows)],
        frow.at[:, pl.ds(pl.multiple_of(c * width, 128), width)],
        own_sem.at[1],
    )
    own_f.start()

    total = gacc[pl.ds(pl.multiple_of(n * piece, 16), piece), :]
    for j in range(1, nodes):
        rs_copy(j).wait_recv()
        total = total + rsbuf[j - 1].astype(jnp.float32)

    def g_rows(node, col):
        return gall.at[pl.ds(pl.multiple_of(col * width + node * piece, 16), piece)]

    gall[pl.ds(pl.multiple_of(c * width + n * piece, 16), piece), :] = total.astype(gall.dtype)

    def ag_copy(dn, dc):
        slot = dn * pairs + dc
        return remote(
            g_rows(n, c), g_rows(n, c), ag_send.at[slot], ag_recv.at[slot],
            wrap(n + dn, nodes), wrap(c + 2 * dc, cols),
        )

    def fw_copy(dn, dc):
        slot = dn * pairs + dc
        rows = g_rows(wrap(n - dn, nodes), wrap(c - 2 * dc, cols))
        return remote(rows, rows, fw_send.at[slot], fw_recv.at[slot], n, sib)

    steps = [(dn, dc) for dn in range(nodes) for dc in range(pairs)]
    fw_copy(0, 0).start()
    for dn, dc in steps[1:]:
        ag_copy(dn, dc).start()
    for dn, dc in steps[1:]:
        ag_copy(dn, dc).wait_recv()
        fw_copy(dn, dc).start()
    own_f.wait()
    for j in range(1, cols):
        f_copy(j).wait_recv()
    for dn, dc in steps:
        fw_copy(dn, dc).wait_recv()

    @pl.when(has_hi)
    def _():
        for k in range(WIDTH):
            up_copy(k).wait_send()
        up_shift().wait_send()

    @pl.when(has_lo)
    def _():
        for k in range(WIDTH):
            down_copy(k).wait_send()
        down_shift().wait_send()

    for j in range(pairs):
        d_copy(j).wait_send()
    for j in range(1, pairs):
        d_forward(j).wait_send()
    for j in range(1, cols):
        f_copy(j).wait_send()
    for j in range(1, nodes):
        rs_copy(j).wait_send()
    for dn, dc in steps[1:]:
        ag_copy(dn, dc).wait_send()
    for dn, dc in steps:
        fw_copy(dn, dc).wait_send()


def finish(cols, frow, gall, gram_ref, rot_ref):
    vecs = gall.shape[0]
    width = vecs // cols
    c = lax.axis_index("cols")
    rotated = lax.dot_general(
        frow[...], gall[...], (((1,), (1,)), ((), ())), preferred_element_type=jnp.float32
    )
    rot_ref[...] = (rotated * vecs ** (-0.5)).astype(rot_ref.dtype)
    unit = (
        lax.broadcasted_iota(jnp.int32, (width, width), 0)
        == lax.broadcasted_iota(jnp.int32, (width, width), 1)
    ).astype(jnp.float32).astype(gall.dtype)
    gram_ref[...] = lax.dot_general(
        unit, gall[:, pl.ds(pl.multiple_of(c * width, 128), width)],
        (((1,), (1,)), ((), ())), preferred_element_type=jnp.float32,
    )


def shards_fused(nodes, cols, vectors, node_shift, coupling, dual_basis):
    layers, dofs, gy, gz, width = vectors.shape
    own_rows, vecs = dual_basis.shape
    slab = layers * dofs * gy * gz
    piece = width // nodes
    pairs = cols // 2
    f32, bf16 = jnp.float32, jnp.bfloat16
    dma = pltpu.SemaphoreType.DMA
    vmem = pl.BlockSpec(memory_space=pltpu.VMEM)
    hbm = pl.BlockSpec(memory_space=pltpu.HBM)
    frow, gall = pl.pallas_call(
        functools.partial(kernel, nodes, cols),
        out_shape=(
            jax.ShapeDtypeStruct((own_rows, vecs), bf16),
            jax.ShapeDtypeStruct((vecs, vecs), bf16),
        ),
        in_specs=[hbm, vmem, pl.BlockSpec(memory_space=pltpu.SMEM), hbm],
        out_specs=(vmem, vmem),
        scratch_shapes=[
            pltpu.VMEM((layers, dofs, gy, gz, width), bf16),
            pltpu.VMEM((2 * WIDTH, dofs, gy, gz, width), bf16),
            pltpu.VMEM((layers + 6, dofs, gy + 2, gz, width), f32),
            pltpu.VMEM((layers + 4, dofs, gy + 2, gz, width), f32),
            pltpu.VMEM((layers + 2, dofs, gy + 2, gz, width), f32),
            pltpu.VMEM((layers + 4, 8, 128), f32),
            pltpu.VMEM((layers + 4, gy, gz, width), f32),
            pltpu.VMEM((slab, vecs), bf16),
            pltpu.VMEM((slab, width), bf16),
            pltpu.VMEM((width, vecs), f32),
            pltpu.VMEM((width, vecs), bf16),
            pltpu.VMEM((nodes - 1, piece, vecs), bf16),
            dma((2 * WIDTH,)), dma((2 * WIDTH,)), dma((2,)), dma((2,)),
            dma((pairs,)), dma((2 * pairs,)), dma((pairs,)), dma((3,)),
            dma((cols - 1,)), dma((cols - 1,)), dma((nodes - 1,)), dma((nodes - 1,)),
            dma((nodes * pairs,)), dma((nodes * pairs,)), dma((nodes * pairs,)), dma((nodes * pairs,)),
        ],
        compiler_params=pltpu.CompilerParams(
            collective_id=0, has_side_effects=True, vmem_limit_bytes=60 * 1024 * 1024
        ),
        cost_estimate=pl.CostEstimate(flops=4 * own_rows * vecs * vecs, bytes_accessed=4 << 20, transcendentals=0),
    )(vectors, jnp.swapaxes(node_shift, 0, 1), coupling, dual_basis)
    return pl.pallas_call(
        functools.partial(finish, cols),
        out_shape=(
            jax.ShapeDtypeStruct((vecs // cols, vecs), f32),
            jax.ShapeDtypeStruct((own_rows, vecs), bf16),
        ),
        in_specs=[vmem, vmem],
        out_specs=(vmem, vmem),
        compiler_params=pltpu.CompilerParams(vmem_limit_bytes=60 * 1024 * 1024),
        cost_estimate=pl.CostEstimate(flops=2 * own_rows * vecs * vecs, bytes_accessed=2 << 20, transcendentals=0),
    )(frow, gall)


def shards(nodes, cols, vectors, node_shift, coupling, dual_basis):
    layers, dofs, gy, gz, width = vectors.shape
    own_rows = dual_basis.shape[0]
    fits = (
        width % (16 * nodes) == 0 and width % 128 == 0 and gz == 16 and gy <= 8 and layers >= WIDTH
        and cols % 2 == 0 and own_rows % 16 == 0 and own_rows * cols == layers * dofs * gy * gz
    )
    if fits:
        return shards_fused(nodes, cols, vectors, node_shift, coupling, dual_basis)
    return shards_plain(vectors, node_shift, coupling, dual_basis)


def solution(mesh):
    placed = (
        P("nodes", None, None, None, "cols"),
        P("nodes", None, None),
        P(),
        P(("nodes", "cols"), None),
    )
    return jax.shard_map(
        functools.partial(shards, mesh.shape["nodes"], mesh.shape["cols"]),
        mesh=mesh,
        in_specs=placed,
        out_specs=(P("cols", None), P(("nodes", "cols"), None)),
        check_vma=False,
    )
```

```python
import functools

import jax
import jax.numpy as jnp
from jax import lax
from jax.experimental import pallas as pl
from jax.experimental.pallas import tpu as pltpu
from jax.sharding import PartitionSpec as P

center_value = 10.0
half_width = 7.0
MESH = pl.DeviceIdType.MESH
WIDTH = 3


def with_halo(block, sides, width):
    for axis, dim in sides:
        count = lax.axis_size(axis)
        forward = [(i, i + 1) for i in range(count - 1)]
        backward = [(target, source) for source, target in forward]
        low = lax.ppermute(
            lax.slice_in_dim(block, block.shape[dim] - width, None, axis=dim), axis, forward
        )
        high = lax.ppermute(lax.slice_in_dim(block, 0, width, axis=dim), axis, backward)
        block = jnp.concatenate([low, block, high], axis=dim)
    return block


def operate_inner(padded, shift_part, coupling):
    middle = padded[1:-1]
    beside = padded[2:] + padded[:-2]
    spread = jnp.pad(middle, ((0, 0), (0, 0), (1, 1), (1, 1), (0, 0)))
    beside = beside + spread[:, :, 2:, 1:-1] + spread[:, :, :-2, 1:-1]
    beside = beside + spread[:, :, 1:-1, 2:] + spread[:, :, 1:-1, :-2]
    coupled = jnp.einsum("de,xeyzc->xdyzc", coupling, middle, precision=lax.Precision.HIGHEST)
    return (6.0 + shift_part[:, None, :, :, None]) * middle - beside + coupled


def shards_plain(vectors, node_shift, coupling, dual_basis):
    shift_full = node_shift.astype(jnp.float32)

    def advance(state):
        padded = with_halo(state, (("nodes", 0),), 1)
        return operate_inner(padded, shift_full, coupling) - center_value * state

    state_zero = vectors.astype(jnp.float32)
    state_one = advance(state_zero) / half_width
    state_two = 2.0 * advance(state_one) / half_width - state_zero
    state_three = 2.0 * advance(state_two) / half_width - state_one
    filtered = state_three.astype(jnp.bfloat16).reshape(-1, state_three.shape[-1])
    row_stack = lax.all_to_all(filtered, "cols", split_axis=0, concat_axis=1, tiled=True)
    partial_gram = lax.dot_general(
        dual_basis, row_stack, (((0,), (0,)), ((), ())), preferred_element_type=jnp.float32
    )
    vector_count = dual_basis.shape[1]
    own_rows = lax.psum_scatter(partial_gram, "cols", scatter_dimension=0, tiled=True)
    own_rows = lax.psum(own_rows, "nodes")
    rotated_sum = jnp.dot(
        row_stack,
        lax.all_gather(own_rows.astype(jnp.bfloat16), "cols", axis=0, tiled=True),
        preferred_element_type=jnp.float32,
    )
    rotated = (rotated_sum * vector_count ** (-0.5)).astype(jnp.bfloat16)
    return (own_rows, rotated)


def remote(src, dst, send, recv, node, col):
    return pltpu.make_async_remote_copy(
        src_ref=src, dst_ref=dst, send_sem=send, recv_sem=recv,
        device_id=(node, col), device_id_type=MESH,
    )


def kernel(
    nodes, cols, v_hbm, shift_ref, c_ref, d_hbm, frow, gall,
    v_ref, ghost, s0, s1, s2, shc, shb, dall, filt, gacc, gsend, rsbuf,
    halo_send, halo_recv, sh_send, sh_recv, d_send, d_recv, df_send, own_sem,
    f_send, f_recv, rs_send, rs_recv, ag_send, ag_recv, fw_send, fw_recv,
):
    n = lax.axis_index("nodes")
    c = lax.axis_index("cols")
    layers, dofs, gy, gz, width = v_ref.shape
    slab_rows = dofs * gy * gz
    own_rows, vecs = d_hbm.shape
    piece = width // nodes
    sib = c + 1 - 2 * lax.rem(c, 2)
    pairs = cols // 2
    has_lo = n > 0
    has_hi = n < nodes - 1

    def wrap(value, count):
        return lax.rem(value + count, count)

    barrier = pltpu.get_barrier_semaphore()
    partners = []
    for dn in range(nodes):
        for dc in range(pairs):
            if dn or dc:
                partners.append((wrap(n + dn, nodes), wrap(c + 2 * dc, cols)))
    for dc in range(pairs):
        partners.append((n, wrap(sib + 2 * dc, cols)))
    for partner in partners:
        pl.semaphore_signal(barrier, inc=1, device_id=partner, device_id_type=MESH)

    own_v = pltpu.make_async_copy(v_hbm, v_ref, own_sem.at[2])
    own_v.start()
    own_d = pltpu.make_async_copy(
        d_hbm, dall.at[pl.ds(pl.multiple_of(c * own_rows, 16), own_rows)], own_sem.at[0]
    )
    own_d.start()
    shc[2:layers + 2] = jnp.zeros_like(shc[2:layers + 2])
    for l in range(layers):
        shc[l + 2, 0:gy, 0:gz] = shift_ref[:, l].astype(jnp.float32)
    s0[:, :, 0] = jnp.zeros_like(s0[:, :, 0])
    s0[:, :, gy + 1] = jnp.zeros_like(s0[:, :, 0])
    s1[:, :, 0] = jnp.zeros_like(s1[:, :, 0])
    s1[:, :, gy + 1] = jnp.zeros_like(s1[:, :, 0])
    s2[:, :, 0] = jnp.zeros_like(s2[:, :, 0])
    s2[:, :, gy + 1] = jnp.zeros_like(s2[:, :, 0])

    @pl.when(jnp.logical_not(has_lo))
    def _():
        s0[0:3] = jnp.zeros_like(s0[0:3])
        s1[0:2] = jnp.zeros_like(s1[0:2])
        s2[0:1] = jnp.zeros_like(s2[0:1])

    @pl.when(jnp.logical_not(has_hi))
    def _():
        s0[layers + 3:] = jnp.zeros_like(s0[0:3])
        s1[layers + 2:] = jnp.zeros_like(s1[0:2])
        s2[layers + 1:] = jnp.zeros_like(s2[0:1])

    row_id = lax.broadcasted_iota(jnp.int32, (gz, width), 0)
    eye = lax.broadcasted_iota(jnp.int32, (gz, gz), 0) == lax.broadcasted_iota(jnp.int32, (gz, gz), 1)

    def spread(l):
        for y in range(gy):
            row = jnp.broadcast_to(shc[l + 2, y:y + 1, 0:gz], (gz, gz))
            column = jnp.sum(jnp.where(eye, row, 0.0), axis=1, keepdims=True)
            shb[l + 2, y] = jnp.broadcast_to(column + (6.0 - center_value), (gz, width))

    def load(target, block):
        s0[target, :, 1:gy + 1] = block.astype(jnp.float32)

    def beside(mid):
        down = jnp.where(row_id > 0, pltpu.roll(mid, 1, 0), 0.0)
        up = jnp.where(row_id < gz - 1, pltpu.roll(mid, gz - 1, 0), 0.0)
        return down + up

    coef = [[c_ref[d, e] for e in range(dofs)] for d in range(dofs)]

    def stencil(src, at, l, scale, y):
        mids = [src[at, e, y + 1] for e in range(dofs)]
        base = shb[l + 2, y]
        out = []
        for d in range(dofs):
            near = src[at - 1, d, y + 1] + src[at + 1, d, y + 1]
            near = near + (src[at, d, y] + src[at, d, y + 2]) + beside(mids[d])
            total = (base + coef[d][d]) * mids[d] - near
            for e in range(dofs):
                if e != d:
                    total = total + coef[d][e] * mids[e]
            out.append(total * scale)
        return out

    def one(l):
        @pl.loop(0, gy)
        def _(y):
            for d, value in enumerate(stencil(s0, l + 3, l, 1.0 / half_width, y)):
                s1[l + 2, d, y + 1] = value

    def two(l):
        @pl.loop(0, gy)
        def _(y):
            for d, value in enumerate(stencil(s1, l + 2, l, 2.0 / half_width, y)):
                s2[l + 1, d, y + 1] = value - s0[l + 3, d, y + 1]

    def three(l):
        @pl.loop(0, gy)
        def _(y):
            for d, value in enumerate(stencil(s2, l + 1, l, 2.0 / half_width, y)):
                value = value - s1[l + 2, d, y + 1]
                at = pl.multiple_of(l * slab_rows + (d * gy + y) * gz, 16)
                filt[pl.ds(at, gz), :] = value.astype(filt.dtype)

    inner = range(1, layers - 1)
    ends = (0, layers - 1)

    own_v.wait()
    for l in range(layers):
        load(l + 3, v_ref[l])
        spread(l)
    own_d.wait()
    for l in inner:
        one(l)
    pl.semaphore_wait(barrier, len(partners))

    def up_copy(k):
        return remote(v_ref.at[layers - 1 - k], ghost.at[k], halo_send.at[k], halo_recv.at[k], n + 1, c)

    def down_copy(k):
        return remote(
            v_ref.at[k], ghost.at[WIDTH + k], halo_send.at[WIDTH + k], halo_recv.at[WIDTH + k], n - 1, c
        )

    def up_shift():
        return remote(shc.at[pl.ds(layers, 2)], shc.at[pl.ds(0, 2)], sh_send.at[0], sh_recv.at[0], n + 1, c)

    def down_shift():
        return remote(
            shc.at[pl.ds(2, 2)], shc.at[pl.ds(layers + 2, 2)], sh_send.at[1], sh_recv.at[1], n - 1, c
        )

    @pl.when(has_hi)
    def _():
        up_copy(0).start()
        up_shift().start()

    @pl.when(has_lo)
    def _():
        down_copy(0).start()
        down_shift().start()

    for k in range(1, WIDTH):
        @pl.when(has_hi)
        def _(k=k):
            up_copy(k).start()

        @pl.when(has_lo)
        def _(k=k):
            down_copy(k).start()

    def d_rows(q):
        return dall.at[pl.ds(pl.multiple_of(q * own_rows, 16), own_rows)]

    def d_copy(j):
        target = sib if j == 0 else wrap(c + 2 * j, cols)
        return remote(d_rows(c), d_rows(c), d_send.at[j], d_recv.at[j], n, target)

    def d_forward(j):
        source = wrap(c - 2 * j, cols)
        return remote(d_rows(source), d_rows(source), df_send.at[j], d_recv.at[pairs + j], n, sib)

    for j in list(range(1, pairs)) + [0]:
        d_copy(j).start()

    @pl.when(has_lo)
    def _():
        up_copy(0).wait_recv()
        load(2, ghost[0])
        up_shift().wait_recv()
        spread(-1)
        spread(-2)

    @pl.when(has_hi)
    def _():
        down_copy(0).wait_recv()
        load(layers + 3, ghost[WIDTH])
        down_shift().wait_recv()
        spread(layers)
        spread(layers + 1)

    for l in ends:
        one(l)
    for l in inner:
        two(l)

    @pl.when(has_lo)
    def _():
        up_copy(1).wait_recv()
        load(1, ghost[1])
        one(-1)

    @pl.when(has_hi)
    def _():
        down_copy(1).wait_recv()
        load(layers + 4, ghost[WIDTH + 1])
        one(layers)

    for l in ends:
        two(l)
    for l in inner:
        three(l)

    for j in range(1, pairs):
        d_copy(j).wait_recv()
        d_forward(j).start()

    @pl.when(has_lo)
    def _():
        up_copy(2).wait_recv()
        load(0, ghost[2])
        one(-2)
        two(-1)

    @pl.when(has_hi)
    def _():
        down_copy(2).wait_recv()
        load(layers + 5, ghost[WIDTH + 2])
        one(layers + 1)
        two(layers)

    for l in ends:
        three(l)

    def f_copy(j):
        target = wrap(c + j, cols)
        return remote(
            filt.at[pl.ds(pl.multiple_of(target * own_rows, 16), own_rows)],
            frow.at[:, pl.ds(pl.multiple_of(c * width, 128), width)],
            f_send.at[j - 1], f_recv.at[j - 1], n, target,
        )

    for j in range(1, cols):
        f_copy(j).start()
    own_f = pltpu.make_async_copy(
        filt.at[pl.ds(pl.multiple_of(c * own_rows, 16), own_rows)],
        frow.at[:, pl.ds(pl.multiple_of(c * width, 128), width)],
        own_sem.at[1],
    )
    own_f.start()

    d_copy(0).wait_recv()
    for j in range(1, pairs):
        d_forward(j).wait_recv()
    gacc[...] = lax.dot_general(
        filt[...], dall[...], (((0,), (0,)), ((), ())), preferred_element_type=jnp.float32
    )
    gsend[...] = gacc[...].astype(gsend.dtype)

    def rs_copy(j):
        target = wrap(n + j, nodes)
        return remote(
            gsend.at[pl.ds(pl.multiple_of(target * piece, 16), piece)],
            rsbuf.at[j - 1], rs_send.at[j - 1], rs_recv.at[j - 1], target, c,
        )

    for j in range(1, nodes):
        rs_copy(j).start()

    total = gacc[pl.ds(pl.multiple_of(n * piece, 16), piece), :]
    for j in range(1, nodes):
        rs_copy(j).wait_recv()
        total = total + rsbuf[j - 1].astype(jnp.float32)

    def g_rows(node, col):
        return gall.at[pl.ds(pl.multiple_of(col * width + node * piece, 16), piece)]

    gall[pl.ds(pl.multiple_of(c * width + n * piece, 16), piece), :] = total.astype(gall.dtype)

    def ag_copy(dn, dc):
        slot = dn * pairs + dc
        return remote(
            g_rows(n, c), g_rows(n, c), ag_send.at[slot], ag_recv.at[slot],
            wrap(n + dn, nodes), wrap(c + 2 * dc, cols),
        )

    def fw_copy(dn, dc):
        slot = dn * pairs + dc
        rows = g_rows(wrap(n - dn, nodes), wrap(c - 2 * dc, cols))
        return remote(rows, rows, fw_send.at[slot], fw_recv.at[slot], n, sib)

    steps = [(dn, dc) for dn in range(nodes) for dc in range(pairs)]
    fw_copy(0, 0).start()
    for dn, dc in steps[1:]:
        ag_copy(dn, dc).start()
    for dn, dc in steps[1:]:
        ag_copy(dn, dc).wait_recv()
        fw_copy(dn, dc).start()
    own_f.wait()
    for j in range(1, cols):
        f_copy(j).wait_recv()
    for dn, dc in steps:
        fw_copy(dn, dc).wait_recv()

    @pl.when(has_hi)
    def _():
        for k in range(WIDTH):
            up_copy(k).wait_send()
        up_shift().wait_send()

    @pl.when(has_lo)
    def _():
        for k in range(WIDTH):
            down_copy(k).wait_send()
        down_shift().wait_send()

    for j in range(pairs):
        d_copy(j).wait_send()
    for j in range(1, pairs):
        d_forward(j).wait_send()
    for j in range(1, cols):
        f_copy(j).wait_send()
    for j in range(1, nodes):
        rs_copy(j).wait_send()
    for dn, dc in steps[1:]:
        ag_copy(dn, dc).wait_send()
    for dn, dc in steps:
        fw_copy(dn, dc).wait_send()


def finish(cols, frow, gall, gram_ref, rot_ref):
    vecs = gall.shape[0]
    width = vecs // cols
    c = lax.axis_index("cols")
    rotated = lax.dot_general(
        frow[...], gall[...], (((1,), (1,)), ((), ())), preferred_element_type=jnp.float32
    )
    rot_ref[...] = (rotated * vecs ** (-0.5)).astype(rot_ref.dtype)
    unit = (
        lax.broadcasted_iota(jnp.int32, (width, width), 0)
        == lax.broadcasted_iota(jnp.int32, (width, width), 1)
    ).astype(jnp.float32).astype(gall.dtype)
    gram_ref[...] = lax.dot_general(
        unit, gall[:, pl.ds(pl.multiple_of(c * width, 128), width)],
        (((1,), (1,)), ((), ())), preferred_element_type=jnp.float32,
    )


def shards_fused(nodes, cols, vectors, node_shift, coupling, dual_basis):
    layers, dofs, gy, gz, width = vectors.shape
    own_rows, vecs = dual_basis.shape
    slab = layers * dofs * gy * gz
    piece = width // nodes
    pairs = cols // 2
    f32, bf16 = jnp.float32, jnp.bfloat16
    dma = pltpu.SemaphoreType.DMA
    vmem = pl.BlockSpec(memory_space=pltpu.VMEM)
    hbm = pl.BlockSpec(memory_space=pltpu.HBM)
    frow, gall = pl.pallas_call(
        functools.partial(kernel, nodes, cols),
        out_shape=(
            jax.ShapeDtypeStruct((own_rows, vecs), bf16),
            jax.ShapeDtypeStruct((vecs, vecs), bf16),
        ),
        in_specs=[hbm, vmem, pl.BlockSpec(memory_space=pltpu.SMEM), hbm],
        out_specs=(vmem, vmem),
        scratch_shapes=[
            pltpu.VMEM((layers, dofs, gy, gz, width), bf16),
            pltpu.VMEM((2 * WIDTH, dofs, gy, gz, width), bf16),
            pltpu.VMEM((layers + 6, dofs, gy + 2, gz, width), f32),
            pltpu.VMEM((layers + 4, dofs, gy + 2, gz, width), f32),
            pltpu.VMEM((layers + 2, dofs, gy + 2, gz, width), f32),
            pltpu.VMEM((layers + 4, 8, 128), f32),
            pltpu.VMEM((layers + 4, gy, gz, width), f32),
            pltpu.VMEM((slab, vecs), bf16),
            pltpu.VMEM((slab, width), bf16),
            pltpu.VMEM((width, vecs), f32),
            pltpu.VMEM((width, vecs), bf16),
            pltpu.VMEM((nodes - 1, piece, vecs), bf16),
            dma((2 * WIDTH,)), dma((2 * WIDTH,)), dma((2,)), dma((2,)),
            dma((pairs,)), dma((2 * pairs,)), dma((pairs,)), dma((3,)),
            dma((cols - 1,)), dma((cols - 1,)), dma((nodes - 1,)), dma((nodes - 1,)),
            dma((nodes * pairs,)), dma((nodes * pairs,)), dma((nodes * pairs,)), dma((nodes * pairs,)),
        ],
        compiler_params=pltpu.CompilerParams(
            collective_id=0, has_side_effects=True, vmem_limit_bytes=60 * 1024 * 1024
        ),
        cost_estimate=pl.CostEstimate(flops=4 * own_rows * vecs * vecs, bytes_accessed=4 << 20, transcendentals=0),
    )(vectors, jnp.swapaxes(node_shift, 0, 1), coupling, dual_basis)
    return pl.pallas_call(
        functools.partial(finish, cols),
        out_shape=(
            jax.ShapeDtypeStruct((vecs // cols, vecs), f32),
            jax.ShapeDtypeStruct((own_rows, vecs), bf16),
        ),
        in_specs=[vmem, vmem],
        out_specs=(vmem, vmem),
        compiler_params=pltpu.CompilerParams(vmem_limit_bytes=60 * 1024 * 1024),
        cost_estimate=pl.CostEstimate(flops=2 * own_rows * vecs * vecs, bytes_accessed=2 << 20, transcendentals=0),
    )(frow, gall)


def shards(nodes, cols, vectors, node_shift, coupling, dual_basis):
    layers, dofs, gy, gz, width = vectors.shape
    own_rows = dual_basis.shape[0]
    fits = (
        width % (16 * nodes) == 0 and width % 128 == 0 and gz == 16 and gy <= 8 and layers >= WIDTH
        and cols % 2 == 0 and own_rows % 16 == 0 and own_rows * cols == layers * dofs * gy * gz
    )
    if fits:
        return shards_fused(nodes, cols, vectors, node_shift, coupling, dual_basis)
    return shards_plain(vectors, node_shift, coupling, dual_basis)


def solution(mesh):
    placed = (
        P("nodes", None, None, None, "cols"),
        P("nodes", None, None),
        P(),
        P(("nodes", "cols"), None),
    )
    return jax.shard_map(
        functools.partial(shards, mesh.shape["nodes"], mesh.shape["cols"]),
        mesh=mesh,
        in_specs=placed,
        out_specs=(P("cols", None), P(("nodes", "cols"), None)),
        check_vma=False,
    )
```
